32 devices in a mesh: dp: 4 (over y, x), expert: 8 (over z, core).
Axes of the slice: x: 2, y: 2, z: 4, core: 2. Of those that a mesh axis runs over, the one named last changes fastest.
Arguments:
- tokens: bfloat16 [49152, 2048], P(('dp', 'expert')), may hold values from -6 to 6
- upstream: bfloat16 [49152, 2048], P(('dp', 'expert')), may hold values from -6 to 6
- counts: int32 [512], P(('dp', 'expert')), may hold values from 1 to 96, 30720 in all
- assign: int32 [2, 8], replicated, may hold values from 0 to 15
- gate_weight: bfloat16 [16, 512, 2048], P(None, 'expert', 'dp'), may hold values from -0.125 to 0.125
- up_weight: bfloat16 [16, 512, 2048], P(None, 'expert', 'dp'), may hold values from -0.125 to 0.125
- down_weight: bfloat16 [16, 512, 2048], P(None, 'expert', 'dp'), may hold values from -0.25 to 0.25
Outputs:
- token_grad: bfloat16 [49152, 2048], P(('dp', 'expert'))
- gate_weight_grad: float32 [16, 512, 2048], P(None, 'expert', 'dp')
- up_weight_grad: float32 [16, 512, 2048], P(None, 'expert', 'dp')
- down_weight_grad: float32 [16, 512, 2048], P(None, 'expert', 'dp')
The draws below stay inside these ranges and needn't reach their ends.
Inputs may be any that keep to these rules, and one draw needn't show every extreme that they name: assign[s, i] is the expert used by copy slot i in microstep s; several slots may use the same expert. counts[j] live leading rows in micro-batch j of 96 slots; some micro-batch is full in every draw.
All inputs are finite; a program needn't handle non-finite values. No bound on the sum of `counts` on one device may be relied on, other than what follows from the above.
Results may differ from the reference program's by a relative error of at most 0.012.
Values may be sent and summed in bfloat16 or wider, within the bound.
No kernel may reach another device: no remote copies, remote signals or barrier semaphores. Data moves between devices by JAX's collectives and lax.ppermute only.
A program may use at most 128 MiB of HBM per device.

```python
import math
import jax
import jax.numpy as jnp
import numpy as np
from jax import lax

D = 2048
FF = 512
MICRO = 8
STEPS = 2
ROWS = 96
GROUPS = 8
EXPERTS = 16
TOKENS = 49152
DEVICES = 32


def set_ends(result, key, low, top_value):
    index_at = [jax.random.randint(jax.random.fold_in(key, axis), (), 0, length) for axis, length in enumerate(result.shape)]
    main_axis = result.shape.index(max(result.shape))
    neighbour = index_at[:main_axis] + [(index_at[main_axis] + 1) % result.shape[main_axis]] + index_at[main_axis + 1:]
    return result.at[tuple(index_at)].set(low).at[tuple(neighbour)].set(top_value)


def shard_levels(stream_key, extent, pieces, least, largest):
    loudness, own = 1.0, jax.random.fold_in(stream_key, 6)
    for axis_at, shards_of in pieces:
        draws = jnp.exp(jax.random.uniform(jax.random.fold_in(own, axis_at), (shards_of,), jnp.float32, least / len(pieces), largest / len(pieces)))
        loudness = loudness * jnp.repeat(draws, extent[axis_at] // shards_of).reshape([-1 if axis == axis_at else 1 for axis in range(len(extent))])
    return loudness


def length_profile(count, total, reach, lean):
    loads = [(1 << 20) // math.isqrt(grade ** lean) + 1 for grade in range(2, count + 1)]
    rest, given = total - reach - (count - 1), [1] * (count - 1)
    while rest > 0:
        movable = [i for i in range(count - 1) if given[i] < reach]
        mass, remaining = sum([loads[i] for i in movable]), rest
        for i in movable:
            addition = min(reach - given[i], max(1, remaining * loads[i] // mass), rest)
            given[i] = given[i] + addition
            rest = rest - addition
    return np.array([reach] + given)


def ragged_sizes(key, amount, total, reach, slope):
    if amount == 2:
        one = jax.random.randint(key, (), max(1, total - reach), min(reach, total - 1) + 1)
        return jnp.stack([one, total - one])
    tallies = jnp.asarray(length_profile(amount, total, reach, slope), jnp.int32)
    twos = (amount - 1) // 2
    donor, sink = tallies[1:1 + 2 * twos:2], tallies[2:2 + 2 * twos:2]
    slack = jnp.minimum(donor - 1, reach - sink)
    passed = jax.random.randint(jax.random.fold_in(key, 1), (twos,), 0, 1 << 20) % (slack + 1)
    tallies = tallies.at[1:1 + 2 * twos:2].set(donor - passed).at[2:2 + 2 * twos:2].set(sink + passed)
    return tallies[jax.random.permutation(jax.random.fold_in(key, 2), amount)]


def centred(key, dims, deviation, most, pieces=(), kind=jnp.bfloat16):
    entries = jax.random.normal(key, dims, jnp.float32) * deviation
    if len(pieces) > 0:
        entries = shard_levels(key, dims, pieces, -0.22, 0.18) * entries
    return jnp.clip(entries, min=-most, max=most).astype(kind)


def setup_inputs(seed: int = 0) -> dict:
    key_of = jax.random.split(jax.random.key(seed), 8)
    return {
        "tokens": centred(key_of[0], (TOKENS, D), 1.0, 6.0, ((0, 32),)),
        "upstream": centred(key_of[1], (TOKENS, D), 1.0, 6.0, ((0, 32),)),
        "counts": ragged_sizes(key_of[2], DEVICES * STEPS * MICRO, DEVICES * STEPS * MICRO * ROWS * 5 // 8, ROWS, 2).astype(jnp.int32),
        "assign": set_ends(jax.random.randint(key_of[3], (STEPS, GROUPS), 0, EXPERTS), jax.random.fold_in(key_of[3], 1), 0, EXPERTS - 1).astype(jnp.int32),
        "gate_weight": centred(key_of[4], (EXPERTS, FF, D), D ** -0.5, 0.125, ((1, 8), (2, 4))),
        "up_weight": centred(key_of[5], (EXPERTS, FF, D), D ** -0.5, 0.125, ((1, 8), (2, 4))),
        "down_weight": centred(key_of[6], (EXPERTS, FF, D), FF ** -0.5, 0.25, ((1, 8), (2, 4))),
    }


def expert_backward(token_rows, upstream_rows, live_rows, gate_full, up_full, down_full, grad_scale):
    contract_last = (((1,), (1,)), ((), ()))
    contract_first = (((0,), (0,)), ((), ()))
    gate_pre = lax.dot_general(token_rows, gate_full, contract_last, preferred_element_type=jnp.float32)
    up_pre = lax.dot_general(token_rows, up_full, contract_last, preferred_element_type=jnp.float32)
    sigmoid = jax.nn.sigmoid(gate_pre)
    active = gate_pre * sigmoid
    hidden = (active * up_pre).astype(jnp.bfloat16)
    masked = jnp.where(live_rows[:, None], upstream_rows, jnp.zeros_like(upstream_rows))
    hidden_grad = lax.dot_general(masked, down_full, contract_last, preferred_element_type=jnp.float32)
    gate_grad = (hidden_grad * up_pre * sigmoid * (1.0 + gate_pre * (1.0 - sigmoid))).astype(jnp.bfloat16)
    up_grad = (hidden_grad * active).astype(jnp.bfloat16)
    input_grad = jnp.dot(gate_grad, gate_full, preferred_element_type=jnp.float32) + jnp.dot(up_grad, up_full, preferred_element_type=jnp.float32)
    gate_term = lax.dot_general(gate_grad, token_rows, contract_first, preferred_element_type=jnp.float32) * grad_scale
    up_term = lax.dot_general(up_grad, token_rows, contract_first, preferred_element_type=jnp.float32) * grad_scale
    down_term = lax.dot_general(hidden, masked, contract_first, preferred_element_type=jnp.float32) * grad_scale
    return input_grad.astype(jnp.bfloat16), gate_term, up_term, down_term


def round_trip(value):
    return lax.optimization_barrier(value.astype(jnp.bfloat16)).astype(jnp.float32)


def reference(tokens, upstream, counts, assign, gate_weight, up_weight, down_weight):
    block_rows = MICRO * ROWS
    grad_scale = 1.0 / block_rows
    token_blocks = tokens.reshape(DEVICES, STEPS, block_rows, D)
    upstream_blocks = upstream.reshape(DEVICES, STEPS, block_rows, D)
    count_blocks = counts.reshape(DEVICES, STEPS, MICRO)
    device_slot = (jnp.arange(DEVICES, dtype=jnp.int32) % GROUPS).astype(jnp.int32)
    position = jnp.arange(ROWS, dtype=jnp.int32)

    def visit_device(totals, inputs):
        token_dev, upstream_dev, count_dev, slot_index = inputs
        gate_total, up_total, down_total = totals
        produced = []
        for micro_step in range(STEPS):
            chosen = assign[micro_step, slot_index].astype(jnp.int32)
            live_rows = (position[None, :] < count_dev[micro_step][:, None]).reshape(block_rows)
            input_grad, gate_term, up_term, down_term = expert_backward(
                token_dev[micro_step], upstream_dev[micro_step], live_rows,
                gate_weight[chosen], up_weight[chosen], down_weight[chosen], grad_scale)
            gate_total = gate_total.at[chosen].add(round_trip(gate_term))
            up_total = up_total.at[chosen].add(round_trip(up_term))
            down_total = down_total.at[chosen].add(round_trip(down_term))
            produced.append(input_grad)
        return (gate_total, up_total, down_total), jnp.stack(produced)

    empty_grad = jnp.zeros((EXPERTS, FF, D), jnp.float32)
    totals, token_grad = lax.scan(visit_device, (empty_grad, empty_grad, empty_grad),
                                  (token_blocks, upstream_blocks, count_blocks, device_slot))
    return token_grad.reshape(TOKENS, D), totals[0], totals[1], totals[2]
```

```python
import functools

import jax
import jax.numpy as jnp
from jax import lax
from jax.experimental import pallas as pl
from jax.experimental.pallas import tpu as pltpu
from jax.sharding import PartitionSpec as P

VMEM_BYTES = 56 * 1024 * 1024
ANY = pl.BlockSpec(memory_space=pl.ANY)
SMEM = pl.BlockSpec(memory_space=pltpu.SMEM)
VMEM = pl.BlockSpec(memory_space=pltpu.VMEM)


def exchange(value, axis, mask):
    size = lax.axis_size(axis)
    return lax.ppermute(value, axis, [(i, i ^ mask) for i in range(size)])


def axis_bits(size):
    return [1 << b for b in range(size.bit_length() - 1)]


def params(**extra):
    return pltpu.CompilerParams(vmem_limit_bytes=VMEM_BYTES, **extra)


def cost(flops, nbytes, trans=0):
    return pl.CostEstimate(flops=flops, bytes_accessed=nbytes, transcendentals=trans)


def pick_kernel(assign, gate, up, down, *rest):
    outs, sems = rest[:-1], rest[-1]
    steps, slots = assign.shape
    me = lax.axis_index("expert")
    copies = []
    for s in range(steps):
        for k in range(slots):
            chosen = assign[s, jnp.bitwise_xor(me, k)]
            for w, ref in enumerate((gate, up, down)):
                n = s * slots + k
                copy = pltpu.make_async_copy(ref.at[chosen], outs[n].at[w], sems.at[n, w])
                copy.start()
                copies.append(copy)
    for copy in copies:
        copy.wait()


def pick(assign, gate, up, down):
    steps, slots = assign.shape
    piece = jax.ShapeDtypeStruct((3,) + gate.shape[1:], gate.dtype)
    flat = pl.pallas_call(
        pick_kernel,
        out_shape=[piece] * (steps * slots),
        in_specs=[SMEM, ANY, ANY, ANY],
        out_specs=[ANY] * (steps * slots),
        scratch_shapes=[pltpu.SemaphoreType.DMA((steps * slots, 3))],
        compiler_params=params(),
        name="pick",
    )(assign, gate, up, down)
    return [flat[s * slots : (s + 1) * slots] for s in range(steps)]


def spread(own, order):
    have = {0: own}
    for bit in order:
        for j in list(have):
            have[j ^ bit] = exchange(have[j], "dp", bit)
    return have


def gather_rows(pieces, me, target, sems, first):
    copies = []
    kept = target.shape[0]
    for n, (j, row, ref) in enumerate(pieces):
        rows, columns = ref.shape[1], ref.shape[2]
        at = pl.multiple_of(jnp.bitwise_xor(me, j) * columns, columns)
        copies.append(
            pltpu.make_async_copy(
                ref.at[pl.ds(0, kept)],
                target.at[:, pl.ds(row, rows), pl.ds(at, columns)],
                sems.at[first + n],
            )
        )
    return copies


CONTRACT_LAST = (((1,), (1,)), ((), ()))
CONTRACT_FIRST = (((0,), (0,)), ((), ()))


def act_kernel(step, batches, places, counts, tokens, upstream, *rest):
    refs = rest[: len(places)]
    hidden, gate_grad, up_grad, weights, x, g, pre, sems = rest[len(places) :]
    me = lax.axis_index("dp")
    rows = x.shape[0]
    pieces = [(j, row, ref) for (j, row), ref in zip(places, refs)]
    loads = [
        pltpu.make_async_copy(tokens.at[pl.ds(step * rows, rows)], x, sems.at[0]),
        pltpu.make_async_copy(upstream.at[pl.ds(step * rows, rows)], g, sems.at[1]),
    ] + gather_rows(pieces, me, weights, sems, 2)
    for load in loads:
        load.start()
    for load in loads:
        load.wait()
    width = pre.shape[2]
    batch_rows = rows // batches
    for at in range(0, hidden.shape[1], width):
        cols = pl.ds(at, width)
        for w, left in enumerate((x, x, g)):
            pre[w] = lax.dot_general(
                left[...], weights[w, cols, :], CONTRACT_LAST, preferred_element_type=jnp.float32
            )
        for b in range(batches):
            span = pl.ds(b * batch_rows, batch_rows)
            live = (
                lax.broadcasted_iota(jnp.int32, (batch_rows, width), 0)
                < counts[step * batches + b]
            )
            gate_pre, up_pre, hidden_grad = pre[0, span, :], pre[1, span, :], pre[2, span, :]
            sigmoid = jax.nn.sigmoid(gate_pre)
            active = gate_pre * sigmoid
            kept = jnp.where(live, hidden_grad, 0.0)
            hidden[span, cols] = jnp.where(live, active * up_pre, 0.0).astype(hidden.dtype)
            gate_grad[span, cols] = (
                kept * up_pre * sigmoid * (1.0 + gate_pre * (1.0 - sigmoid))
            ).astype(gate_grad.dtype)
            up_grad[span, cols] = (kept * active).astype(up_grad.dtype)


def act(step, rows, batches, counts, tokens, upstream, placed):
    features = tokens.shape[1]
    places = tuple((j, row) for j, row, _ in placed)
    arrays = [a for _, _, a in placed]
    units = sum(a.shape[1] * a.shape[2] for a in arrays) // features
    out = jax.ShapeDtypeStruct((rows, units), tokens.dtype)
    width = min(units, 256)
    return pl.pallas_call(
        functools.partial(act_kernel, step, batches, places),
        out_shape=[out] * 3,
        in_specs=[SMEM, ANY, ANY] + [ANY] * len(arrays),
        out_specs=[VMEM] * 3,
        scratch_shapes=[
            pltpu.VMEM((3, units, features), tokens.dtype),
            pltpu.VMEM((rows, features), tokens.dtype),
            pltpu.VMEM((rows, features), tokens.dtype),
            pltpu.VMEM((3, rows, width), jnp.float32),
            pltpu.SemaphoreType.DMA((2 + len(arrays),)),
        ],
        compiler_params=params(),
        cost_estimate=cost(
            6 * rows * units * features, 2 * (2 * rows + 3 * units) * features, rows * units
        ),
        name="act",
    )(counts, tokens, upstream, *arrays)


def weight_grads_kernel(step, scale, layout, tokens, upstream, hidden, gate_grad, up_grad, *rest):
    outs = rest[: len(layout)]
    x, g, turned, stage, sems = rest[len(layout) :]
    parts, rows, width = x.shape
    me = lax.axis_index("dp")
    order = list(range(parts))[::-1]
    loads = {}
    for j in order:
        at = pl.multiple_of(jnp.bitwise_xor(me, j) * width, width)
        for n, (whole, local) in enumerate(((tokens, x), (upstream, g))):
            loads[j, n] = pltpu.make_async_copy(
                whole.at[pl.ds(step * rows, rows), pl.ds(at, width)],
                local.at[j],
                sems.at[2 * j + n],
            )
            loads[j, n].start()
    for w, ref in enumerate((gate_grad, up_grad, hidden)):
        turned[w] = ref[...].T
    stores = []
    for j in order:
        for w in range(3):
            if w == 0:
                loads[j, 0].wait()
            if w == 2:
                loads[j, 1].wait()
            right = (x, x, g)[w]
            stage[j, w] = (
                jnp.dot(turned[w], right[j], preferred_element_type=jnp.float32) * scale
            ).astype(stage.dtype)
        for n, (jj, row) in enumerate(layout):
            if jj == j:
                store = pltpu.make_async_copy(
                    stage.at[j, :, pl.ds(row, outs[n].shape[1]), :],
                    outs[n],
                    sems.at[2 * parts + n],
                )
                store.start()
                stores.append(store)
    for store in stores:
        store.wait()


def weight_grads(step, parts, scale, tokens, upstream, hidden, gate_grad, up_grad, layout, sizes):
    rows, units = hidden.shape
    features = tokens.shape[1]
    width = features // parts
    return pl.pallas_call(
        functools.partial(weight_grads_kernel, step, scale, layout),
        out_shape=[jax.ShapeDtypeStruct((3, size, width), tokens.dtype) for size in sizes],
        in_specs=[ANY, ANY, VMEM, VMEM, VMEM],
        out_specs=[ANY] * len(sizes),
        scratch_shapes=[
            pltpu.VMEM((parts, rows, width), tokens.dtype),
            pltpu.VMEM((parts, rows, width), tokens.dtype),
            pltpu.VMEM((3, units, rows), tokens.dtype),
            pltpu.VMEM((parts, 3, units, width), tokens.dtype),
            pltpu.SemaphoreType.DMA((2 * parts + len(sizes),)),
        ],
        compiler_params=params(),
        cost_estimate=cost(
            6 * rows * units * features, 2 * (2 * rows + 3 * units) * features
        ),
        name="weight_grads",
    )(tokens, upstream, hidden, gate_grad, up_grad)


def input_grad_kernel(step, places, has_base, gate_grad, up_grad, *rest):
    refs = rest[: len(places)]
    out, weights, stage, sems = rest[len(places) + has_base :]
    me = lax.axis_index("dp")
    pieces = [(j, row, ref) for (j, row), ref in zip(places, refs)]
    loads = gather_rows(pieces, me, weights, sems, 0)
    for load in loads:
        load.start()
    for load in loads:
        load.wait()
    parts, rows, width = stage.shape
    stores = []
    for n in range(parts):
        cols = pl.ds(n * width, width)
        stage[n] = (
            jnp.dot(gate_grad[...], weights[0, :, cols], preferred_element_type=jnp.float32)
            + jnp.dot(up_grad[...], weights[1, :, cols], preferred_element_type=jnp.float32)
        ).astype(stage.dtype)
        store = pltpu.make_async_copy(
            stage.at[n], out.at[pl.ds(step * rows, rows), cols], sems.at[len(places) + n]
        )
        store.start()
        stores.append(store)
    for store in stores:
        store.wait()


def input_grad(step, steps, gate_grad, up_grad, placed, features, base):
    rows, units = gate_grad.shape
    places = tuple((j, row) for j, row, _ in placed)
    arrays = [a for _, _, a in placed]
    parts = max(1, features // 512)
    more = [] if base is None else [base]
    return pl.pallas_call(
        functools.partial(input_grad_kernel, step, places, len(more)),
        out_shape=jax.ShapeDtypeStruct((steps * rows, features), gate_grad.dtype),
        in_specs=[VMEM, VMEM] + [ANY] * (len(arrays) + len(more)),
        out_specs=ANY,
        scratch_shapes=[
            pltpu.VMEM((2, units, features), gate_grad.dtype),
            pltpu.VMEM((parts, rows, features // parts), gate_grad.dtype),
            pltpu.SemaphoreType.DMA((len(arrays) + parts,)),
        ],
        input_output_aliases={2 + len(arrays): 0} if more else {},
        compiler_params=params(),
        cost_estimate=cost(4 * rows * units * features, 2 * (rows + 2 * units) * features),
        name="input_grad",
    )(gate_grad, up_grad, *arrays, *more)


def collect(parts, order):
    have = dict(parts)
    for bit in order:
        for j in [j for j in have if j & bit]:
            got = exchange(have.pop(j), "dp", bit)
            mine = have[j ^ bit]
            have[j ^ bit] = (mine.astype(jnp.float32) + got.astype(jnp.float32)).astype(mine.dtype)
    return have[0]


def place_kernel(assign, *rest):
    steps, slots = assign.shape
    pieces = rest[: steps * slots]
    outs = rest[steps * slots :]
    me = lax.axis_index("expert")
    expert = pl.program_id(0)
    for out in outs:
        out[...] = jnp.zeros_like(out)
    for s in range(steps):
        for k in range(slots):

            @pl.when(assign[s, jnp.bitwise_xor(me, k)] == expert)
            def _():
                for w, out in enumerate(outs):
                    out[0] += pieces[s * slots + k][w].astype(jnp.float32)


def place(assign, home, experts):
    _, units, width = home[0].shape
    out = jax.ShapeDtypeStruct((experts, units, width), jnp.float32)
    return pl.pallas_call(
        place_kernel,
        grid=(experts,),
        out_shape=[out] * 3,
        in_specs=[SMEM] + [VMEM] * len(home),
        out_specs=[pl.BlockSpec((1, units, width), lambda e: (e, 0, 0))] * 3,
        compiler_params=params(),
        name="place",
    )(assign, *home)


def local(tokens, upstream, counts, assign, gate_weight, up_weight, down_weight):
    steps, slots = assign.shape
    rows = tokens.shape[0] // steps
    batches = counts.shape[0] // steps
    features = tokens.shape[1]
    experts, chunk, _ = gate_weight.shape
    parts = lax.axis_size("dp")
    bits = axis_bits(parts)
    orders = (bits, bits[::-1])
    even = list(range(0, slots, 2))
    near = [k for k in even if k not in (0, slots // 2)]
    staged = [g for g in ([0], near, [slots // 2]) if g]
    half_units = slots // 2 * chunk

    picked = pick(assign, gate_weight, up_weight, down_weight)
    token_grad = None
    home = [[None] * slots for _ in range(steps)]
    for s in range(steps):
        groups = staged if s == 0 else [even]
        received = [
            picked[s][k] if k == 0 else exchange(picked[s][k], "expert", k) for k in range(slots)
        ]
        placed = []
        for half in range(2):
            for group in groups:
                row = half * half_units + sum(
                    len(before) for before in groups[: groups.index(group)]
                ) * chunk
                mine = [received[k ^ half] for k in group]
                own = mine[0] if len(mine) == 1 else jnp.concatenate(mine, axis=1)
                placed += [(j, row, a) for j, a in spread(own, orders[half]).items()]
        hidden, gate_grad, up_grad = act(s, rows, batches, counts, tokens, upstream, placed)
        kept = [k for group in groups for k in group]
        groups_back = [kept] if s == 0 else [[k] for k in kept]
        if s > 0:
            groups_back = [[k] for k in kept if k == slots // 2] + [
                [k] for k in kept if k not in (0, slots // 2)
            ] + [[0]]
        layout, sizes, names = [], [], []
        for group in groups_back:
            for half in range(2):
                for j in range(parts):
                    layout.append((j, half * half_units + kept.index(group[0]) * chunk))
                    sizes.append(len(group) * chunk)
                    names.append((tuple(group), half, j))
        produced = weight_grads(
            s, parts, 1.0 / rows, tokens, upstream, hidden, gate_grad, up_grad,
            tuple(layout), tuple(sizes),
        )
        by_name = dict(zip(names, produced))
        token_grad = input_grad(s, steps, gate_grad, up_grad, placed, features, token_grad)
        for group in groups_back:
            for half in range(2):
                total = collect(
                    {j: by_name[tuple(group), half, j] for j in range(parts)}, orders[half]
                )
                for n, k in enumerate(group):
                    back = total[:, n * chunk : (n + 1) * chunk]
                    k = k ^ half
                    home[s][k] = back if k == 0 else exchange(back, "expert", k)
    totals = place(assign, [piece for step in home for piece in step], experts)
    return (token_grad, *totals)


def solution(mesh):
    placed = (
        P(("dp", "expert"), None),
        P(("dp", "expert"), None),
        P(("dp", "expert")),
        P(),
        P(None, "expert", "dp"),
        P(None, "expert", "dp"),
        P(None, "expert", "dp"),
    )
    return jax.shard_map(
        local,
        mesh=mesh,
        in_specs=placed,
        out_specs=(
            P(("dp", "expert"), None),
            P(None, "expert", "dp"),
            P(None, "expert", "dp"),
            P(None, "expert", "dp"),
        ),
        check_vma=False,
    )
```

```python
import functools

import jax
import jax.numpy as jnp
from jax import lax
from jax.experimental import pallas as pl
from jax.experimental.pallas import tpu as pltpu
from jax.sharding import PartitionSpec as P

VMEM_BYTES = 56 * 1024 * 1024
ANY = pl.BlockSpec(memory_space=pl.ANY)
SMEM = pl.BlockSpec(memory_space=pltpu.SMEM)
VMEM = pl.BlockSpec(memory_space=pltpu.VMEM)
CONTRACT_LAST = (((1,), (1,)), ((), ()))
KINDS = 3


def xor(a, b):
    return jnp.bitwise_xor(a, b)


def swap(value, mask):
    size = lax.axis_size("expert")
    return lax.ppermute(value, "expert", [(i, i ^ mask) for i in range(size)])


def axis_bits(size):
    return [1 << b for b in range(size.bit_length() - 1)]


def hop(value, turn):
    parts, slots = lax.axis_size("dp"), lax.axis_size("expert")
    bits = axis_bits(parts)
    pairs = []
    for d in range(parts):
        for e in range(slots):
            bit = (bits if e % 2 == 0 else bits[::-1])[turn]
            pairs.append((d * slots + e, (d ^ bit) * slots + e))
    return lax.ppermute(value, ("dp", "expert"), pairs)


def feature_block(parts, j):
    bits = axis_bits(parts)
    even = sum(b for t, b in enumerate(bits) if j >> t & 1)
    odd = sum(b for t, b in enumerate(bits[::-1]) if j >> t & 1)
    mask = jnp.where(lax.axis_index("expert") % 2 == 0, even, odd)
    return xor(lax.axis_index("dp"), mask)


def params():
    return pltpu.CompilerParams(vmem_limit_bytes=VMEM_BYTES)


def cost(flops, nbytes, trans=0):
    return pl.CostEstimate(flops=flops, bytes_accessed=nbytes, transcendentals=trans)


def run(copies):
    for copy in copies:
        copy.start()
    for copy in copies:
        copy.wait()


def pick_kernel(wanted, extra, assign, *rest):
    weights, rest = rest[:KINDS], rest[KINDS:]
    given, outs, sems = rest[:extra], rest[extra:-1], rest[-1]
    me = lax.axis_index("expert")
    copies = []
    for out, chunks in zip(outs, wanted):
        for n, (s, k) in enumerate(chunks):
            if s is None:
                copies.append(pltpu.make_async_copy(given[0].at[k], out.at[n], sems.at[len(copies)]))
                continue
            chosen = assign[s, xor(me, k)]
            for w, ref in enumerate(weights):
                copies.append(
                    pltpu.make_async_copy(ref.at[chosen], out.at[n, w], sems.at[len(copies)])
                )
    run(copies)


def pick(wanted, assign, weights, given=()):
    chunk = (KINDS,) + weights[0].shape[1:]
    dtype = weights[0].dtype
    count = sum(KINDS if s is not None else 1 for chunks in wanted for s, _ in chunks)
    return pl.pallas_call(
        functools.partial(pick_kernel, wanted, len(given)),
        out_shape=[jax.ShapeDtypeStruct((len(chunks),) + chunk, dtype) for chunks in wanted],
        in_specs=[SMEM] + [ANY] * (KINDS + len(given)),
        out_specs=[VMEM] * len(wanted),
        scratch_shapes=[pltpu.SemaphoreType.DMA((count,))],
        compiler_params=params(),
        cost_estimate=cost(0, 4 * sum(map(len, wanted)) * chunk[0] * chunk[1] * chunk[2]),
        name="pick",
    )(assign, *weights, *given)


def weight_loads(pieces, kept, target, sems, first):
    parts = lax.axis_size("dp")
    copies = []
    for ref, n, j, position in pieces:
        units, width = ref.shape[2], ref.shape[3]
        at = pl.multiple_of(feature_block(parts, j) * width, width)
        copies.append(
            pltpu.make_async_copy(
                ref.at[n, pl.ds(0, kept)],
                target.at[:, pl.ds(position * units, units), pl.ds(at, width)],
                sems.at[first + len(copies)],
            )
        )
    return copies


def bind(table, refs):
    return [(refs[a], n, j, position) for a, n, j, position in table]


def act_kernel(step, batches, table, count, counts, tokens, upstream, *rest):
    pieces = bind(table, rest[:count])
    hidden, gate_grad, up_grad, weights, x, g, pre, sems = rest[count:]
    rows = x.shape[0]
    run(
        [
            pltpu.make_async_copy(tokens.at[pl.ds(step * rows, rows)], x, sems.at[0]),
            pltpu.make_async_copy(upstream.at[pl.ds(step * rows, rows)], g, sems.at[1]),
        ]
        + weight_loads(pieces, KINDS, weights, sems, 2)
    )
    width = pre.shape[2]
    batch_rows = rows // batches
    for at in range(0, hidden.shape[1], width):
        cols = pl.ds(at, width)
        for w, left in enumerate((x, x, g)):
            pre[w] = lax.dot_general(
                left[...], weights[w, cols, :], CONTRACT_LAST, preferred_element_type=jnp.float32
            )
        for b in range(batches):
            span = pl.ds(b * batch_rows, batch_rows)
            live = (
                lax.broadcasted_iota(jnp.int32, (batch_rows, width), 0)
                < counts[step * batches + b]
            )
            gate_pre, up_pre, hidden_grad = pre[0, span, :], pre[1, span, :], pre[2, span, :]
            sigmoid = jax.nn.sigmoid(gate_pre)
            active = gate_pre * sigmoid
            kept = jnp.where(live, hidden_grad, 0.0)
            hidden[span, cols] = jnp.where(live, active * up_pre, 0.0).astype(hidden.dtype)
            gate_grad[span, cols] = (
                kept * up_pre * sigmoid * (1.0 + gate_pre * (1.0 - sigmoid))
            ).astype(gate_grad.dtype)
            up_grad[span, cols] = (kept * active).astype(up_grad.dtype)


def act(step, rows, units, batches, counts, tokens, upstream, table, arrays):
    features = tokens.shape[1]
    out = jax.ShapeDtypeStruct((rows, units), tokens.dtype)
    width = min(units, 256)
    return pl.pallas_call(
        functools.partial(act_kernel, step, batches, table, len(arrays)),
        out_shape=[out] * 3,
        in_specs=[SMEM, ANY, ANY] + [ANY] * len(arrays),
        out_specs=[VMEM] * 3,
        scratch_shapes=[
            pltpu.VMEM((KINDS, units, features), tokens.dtype),
            pltpu.VMEM((rows, features), tokens.dtype),
            pltpu.VMEM((rows, features), tokens.dtype),
            pltpu.VMEM((3, rows, width), jnp.float32),
            pltpu.SemaphoreType.DMA((2 + len(table),)),
        ],
        compiler_params=params(),
        cost_estimate=cost(
            6 * rows * units * features, 2 * (2 * rows + 3 * units) * features, rows * units
        ),
        name="act",
    )(counts, tokens, upstream, *arrays)


def weight_grads_kernel(step, scale, groups, tokens, upstream, hidden, gate_grad, up_grad, *rest):
    x, g, turned, stage, sems = rest[-5:]
    outs = rest[:-5]
    parts, rows, width = x.shape
    chunk = outs[0].shape[2]
    order = list(range(parts))[::-1]
    loads = {}
    for j in order:
        at = pl.multiple_of(feature_block(parts, j) * width, width)
        for n, (whole, local) in enumerate(((tokens, x), (upstream, g))):
            loads[j, n] = pltpu.make_async_copy(
                whole.at[pl.ds(step * rows, rows), pl.ds(at, width)],
                local.at[j],
                sems.at[2 * j + n],
            )
            loads[j, n].start()
    for w, ref in enumerate((gate_grad, up_grad, hidden)):
        turned[w] = ref[...].T
    stores = []
    for j in order:
        for w in range(KINDS):
            if w == 0:
                loads[j, 0].wait()
            if w == 2:
                loads[j, 1].wait()
            right = (x, x, g)[w]
            stage[j, w] = (
                jnp.dot(turned[w], right[j], preferred_element_type=jnp.float32) * scale
            ).astype(stage.dtype)
        for n, positions in enumerate(groups):
            for i, position in enumerate(positions):
                store = pltpu.make_async_copy(
                    stage.at[j, :, pl.ds(position * chunk, chunk), :],
                    outs[n * parts + j].at[i],
                    sems.at[2 * parts + len(stores)],
                )
                store.start()
                stores.append(store)
    for store in stores:
        store.wait()


def weight_grads(step, parts, chunk, scale, tokens, upstream, hidden, gate_grad, up_grad, groups):
    rows, units = hidden.shape
    features = tokens.shape[1]
    width = features // parts
    shapes = [
        jax.ShapeDtypeStruct((len(positions), KINDS, chunk, width), tokens.dtype)
        for positions in groups
        for _ in range(parts)
    ]
    stores = sum(map(len, groups)) * parts
    flat = pl.pallas_call(
        functools.partial(weight_grads_kernel, step, scale, groups),
        out_shape=shapes,
        in_specs=[ANY, ANY, VMEM, VMEM, VMEM],
        out_specs=[ANY] * len(shapes),
        scratch_shapes=[
            pltpu.VMEM((parts, rows, width), tokens.dtype),
            pltpu.VMEM((parts, rows, width), tokens.dtype),
            pltpu.VMEM((KINDS, units, rows), tokens.dtype),
            pltpu.VMEM((parts, KINDS, units, width), tokens.dtype),
            pltpu.SemaphoreType.DMA((2 * parts + stores,)),
        ],
        compiler_params=params(),
        cost_estimate=cost(6 * rows * units * features, 2 * (2 * rows + 3 * units) * features),
        name="weight_grads",
    )(tokens, upstream, hidden, gate_grad, up_grad)
    return [
        {j: flat[n * parts + j] for j in range(parts)} for n in range(len(groups))
    ]


def input_grad_kernel(step, table, count, has_base, gate_grad, up_grad, *rest):
    pieces = bind(table, rest[:count])
    out, weights, stage, sems = rest[count + has_base :]
    run(weight_loads(pieces, 2, weights, sems, 0))
    parts, rows, width = stage.shape
    stores = []
    for n in range(parts):
        cols = pl.ds(n * width, width)
        stage[n] = (
            jnp.dot(gate_grad[...], weights[0, :, cols], preferred_element_type=jnp.float32)
            + jnp.dot(up_grad[...], weights[1, :, cols], preferred_element_type=jnp.float32)
        ).astype(stage.dtype)
        store = pltpu.make_async_copy(
            stage.at[n], out.at[pl.ds(step * rows, rows), cols], sems.at[len(table) + n]
        )
        store.start()
        stores.append(store)
    for store in stores:
        store.wait()


def input_grad(step, steps, gate_grad, up_grad, table, arrays, features, base):
    rows, units = gate_grad.shape
    parts = max(1, features // 512)
    more = [] if base is None else [base]
    return pl.pallas_call(
        functools.partial(input_grad_kernel, step, table, len(arrays), len(more)),
        out_shape=jax.ShapeDtypeStruct((steps * rows, features), gate_grad.dtype),
        in_specs=[VMEM, VMEM] + [ANY] * (len(arrays) + len(more)),
        out_specs=ANY,
        scratch_shapes=[
            pltpu.VMEM((2, units, features), gate_grad.dtype),
            pltpu.VMEM((parts, rows, features // parts), gate_grad.dtype),
            pltpu.SemaphoreType.DMA((len(table) + parts,)),
        ],
        input_output_aliases={2 + len(arrays): 0} if more else {},
        compiler_params=params(),
        cost_estimate=cost(4 * rows * units * features, 2 * (rows + 2 * units) * features),
        name="input_grad",
    )(gate_grad, up_grad, *arrays, *more)


def place_kernel(table, count, assign, *rest):
    pieces = rest[:count]
    outs = rest[count:]
    me = lax.axis_index("expert")
    expert = pl.program_id(0)
    for out in outs:
        out[...] = jnp.zeros_like(out)
    for a, n, s, k in table:

        @pl.when(assign[s, xor(me, k)] == expert)
        def _():
            for w, out in enumerate(outs):
                out[0] += pieces[a][n, w].astype(jnp.float32)


def place(assign, home, experts):
    arrays = list({id(a): a for a, _, _, _ in home}.values())
    index = {id(a): i for i, a in enumerate(arrays)}
    table = tuple((index[id(a)], n, s, k) for a, n, s, k in home)
    units, width = arrays[0].shape[2:]
    out = jax.ShapeDtypeStruct((experts, units, width), jnp.float32)
    return pl.pallas_call(
        functools.partial(place_kernel, table, len(arrays)),
        grid=(experts,),
        out_shape=[out] * KINDS,
        in_specs=[SMEM] + [VMEM] * len(arrays),
        out_specs=[pl.BlockSpec((1, units, width), lambda e: (e, 0, 0))] * KINDS,
        compiler_params=params(),
        name="place",
    )(assign, *arrays)


def finish_kernel(table, count, assign, *rest):
    pieces = rest[:count]
    outs = rest[count + KINDS : count + 2 * KINDS]
    held, sems = rest[count + 2 * KINDS :]
    me = lax.axis_index("expert")
    chosen = [assign[s, xor(me, k)] for _, _, s, k in table]
    first = []
    for m in range(len(table)):
        slot = jnp.int32(m)
        for o in range(m - 1, -1, -1):
            slot = jnp.where(chosen[o] == chosen[m], o, slot)
        first.append(slot)
    spots = [(m, w) for m in range(len(table)) for w in range(KINDS)]
    run([pltpu.make_async_copy(outs[w].at[chosen[m]], held.at[m, w], sems.at[m, w]) for m, w in spots])
    for m, (a, n, _, _) in enumerate(table):
        held[first[m]] += pieces[a][n].astype(jnp.float32)
    for wait in (False, True):
        for m in range(len(table)):

            @pl.when(first[m] == m)
            def _():
                for w in range(KINDS):
                    store = pltpu.make_async_copy(
                        held.at[m, w], outs[w].at[chosen[m]], sems.at[m, w]
                    )
                    store.wait() if wait else store.start()


def finish(assign, home, totals):
    arrays = list({id(a): a for a, _, _, _ in home}.values())
    index = {id(a): i for i, a in enumerate(arrays)}
    table = tuple((index[id(a)], n, s, k) for a, n, s, k in home)
    shape = totals[0].shape[1:]
    return pl.pallas_call(
        functools.partial(finish_kernel, table, len(arrays)),
        out_shape=[jax.ShapeDtypeStruct(t.shape, t.dtype) for t in totals],
        in_specs=[SMEM] + [VMEM] * len(arrays) + [ANY] * KINDS,
        out_specs=[ANY] * KINDS,
        scratch_shapes=[
            pltpu.VMEM((len(table), KINDS) + shape, jnp.float32),
            pltpu.SemaphoreType.DMA((len(table), KINDS)),
        ],
        input_output_aliases={1 + len(arrays) + w: w for w in range(KINDS)},
        compiler_params=params(),
        name="finish",
    )(assign, *arrays, *totals)


class Line:
    def __init__(self, depth):
        self.depth = depth
        self.sent = []
        self.gates = {}
        self.plans = []

    def send(self, move, value, *way, behind=()):
        behind = list(behind) + self.gates.get(len(self.sent), [])
        if len(self.sent) >= self.depth:
            behind.append(self.sent[-self.depth])
        if behind:
            value = after(value, *behind)
        self.sent.append(move(value, *way))
        result = self.sent[-1]
        self.settle()
        return result

    def settle(self, everything=False):
        while self.plans and (everything or self.plans[0][0] < len(self.sent)):
            number, plan = self.plans.pop(0)
            plan(self.sent[min(number, len(self.sent) - 1)])

    def plan(self, lag, what):
        self.plans.append((len(self.sent) - 1 + lag, what))
        self.plans.sort(key=lambda item: item[0])


def after(value, *others):
    return lax.optimization_barrier((value, *others))[0]


def overlap(jobs, sends):
    before = None
    for job in jobs:
        next(job)
        if before is not None:
            next(before)
            next(before, None)
        for _ in range(sends - 2):
            next(job)
        before = job
    next(before)
    next(before, None)


def spread(line, own, done):
    have = {0: own}
    for turn in range(len(axis_bits(lax.axis_size("dp")))):
        have[1 << turn] = line.send(hop, own, turn)
        yield True
    for turn in range(len(axis_bits(lax.axis_size("dp")))):
        for j in sorted(have):
            if j and j < 1 << turn:
                have[j | 1 << turn] = line.send(hop, have[j], turn)
                yield True
    done(have)


def collect(line, produced, done):
    terms = {j: [a] for j, a in produced.items()}

    def total(addends):
        if len(addends) == 1:
            return addends[0]
        return sum(a.astype(jnp.float32) for a in addends).astype(addends[0].dtype)

    for turn in range(len(axis_bits(len(produced)))):
        for j in sorted([j for j in terms if j >> turn & 1], reverse=True):
            terms[j ^ 1 << turn].append(line.send(hop, total(terms.pop(j)), turn))
            yield True
    done(total(terms[0]))


def local(tokens, upstream, counts, assign, gate_weight, up_weight, down_weight):
    steps, slots = assign.shape
    rows = tokens.shape[0] // steps
    batches = counts.shape[0] // steps
    features = tokens.shape[1]
    experts, chunk, _ = gate_weight.shape
    parts = lax.axis_size("dp")
    units = slots * chunk
    weights = (gate_weight, up_weight, down_weight)
    every = range(steps)
    far = slots // 2
    near = [k for k in range(2, slots, 2) if k != far]
    remote = near + [far]
    position = {k: 2 * i for i, k in enumerate([0] + remote)}
    wide, deep = Line(3), Line(2)

    own, mate_first, mate_rest = pick(
        (
            tuple((s, 0) for s in every),
            tuple((s, 1) for s in every),
            tuple((s, k ^ 1) for s in every for k in remote),
        ),
        assign,
        weights,
    )
    mate_first = swap(mate_first, 1)
    mate_rest = swap(mate_rest, 1)
    wanted = tuple(
        ((s, k), (None, s * len(remote) + i)) for s in every for i, k in enumerate(remote)
    )
    messages = pick(wanted, assign, weights, (mate_rest,))

    moves = [(s, k) for s in every for k in remote]
    arrived = {}

    def fetch(key):
        while key not in arrived:
            n = len(deep.sent)
            s, k = moves[n]
            at = 2 * n + 1 - len(near) % 2
            behind = wide.sent[min(at, len(wide.sent) - 1) :][:1] if n >= len(near) else ()
            arrived[s, k] = deep.send(swap, messages[n], k, behind=behind)

    def ahead(arrival):
        n = len(deep.sent)
        if n < len(moves) and 2 * n + 1 < len(wide.sent):
            fetch(moves[n])
        wide.plan(1, ahead)

    table = [[] for _ in every]

    def deliver(keys, array, places):
        for key in keys:
            fetch(key)
        if keys:
            pairs = [arrived[key] for key in keys]
            array = pairs[0] if len(pairs) == 1 else jnp.concatenate(pairs)

        def done(have):
            for j, a in have.items():
                for n, (s, p) in enumerate(places):
                    table[s].append((a, n, j, p))

        yield from spread(wide, array, done)

    jobs = [
        deliver([], own, [(s, 0) for s in every]),
        deliver([], mate_first, [(s, 1) for s in every]),
    ]
    for s in every:
        for group in (near, [far]):
            if group:
                places = [(s, position[k] + c) for k in group for c in range(2)]
                jobs.append(deliver([(s, k) for k in group], None, places))
    for k in near:
        fetch((0, k))
    wide.plan(1, ahead)
    overlap(jobs, parts - 1)
    wide.plans.clear()

    token_grad = None
    early, late = [], []
    jobs = []
    for s in every:
        arrays = list({id(a): a for a, _, _, _ in table[s]}.values())
        index = {id(a): i for i, a in enumerate(arrays)}
        places = tuple((index[id(a)], n, j, p) for a, n, j, p in table[s])
        hidden, gate_grad, up_grad = act(
            s, rows, units, batches, counts, tokens, upstream, places, arrays
        )
        groups = [g for g in ([far], near) if g]
        produced = weight_grads(
            s, parts, chunk, 1.0 / rows, tokens, upstream, hidden, gate_grad, up_grad,
            tuple(
                tuple(position[k] + c for k in group for c in range(2)) for group in groups + [[0]]
            ),
        )
        token_grad = input_grad(
            s, steps, gate_grad, up_grad, places, arrays, features, token_grad
        )
        counts = after(counts, token_grad)
        jobs.append([(s, group, terms) for group, terms in zip(groups + [[0]], produced)])

    def returned(s, group):
        home = late if group == [0] or (s == steps - 1 and group != [far]) else early

        def mates(pairs):
            def go(arrival):
                seconds = [pair[1:] for _, pair in pairs]
                seconds = seconds[0] if len(seconds) == 1 else jnp.concatenate(seconds)
                seconds = swap(seconds if arrival is None else after(seconds, arrival), 1)
                home.extend((seconds, n, s, k ^ 1) for n, (k, _) in enumerate(pairs))

            return go

        def done(total):
            pairs = []
            for i, k in enumerate(group):
                pair = total[2 * i : 2 * i + 2]
                if k:
                    pair = deep.send(swap, pair, k)
                home.append((pair, 0, s, k))
                pairs.append((k, pair))
            if group == [0]:
                mates(pairs)(None)
            else:
                wide.plan(parts - 1, mates(pairs))

        return done

    base = len(wide.sent)
    for n in range(parts - 1):
        wide.gates[base + n] = [wide.sent[-1]]
    wide.gates[base + 4 * parts - 6] = [token_grad]
    remote_jobs = [job for step in jobs for job in step[:-1]]
    own_jobs = [step[-1] for step in jobs]
    overlap(
        [
            collect(wide, terms, returned(s, group))
            for s, group, terms in remote_jobs + own_jobs
        ],
        parts - 1,
    )
    wide.settle(True)
    totals = place(after(assign, token_grad), early, experts)
    totals = finish(assign, late, totals)
    return (token_grad, *totals)


def solution(mesh):
    placed = (
        P(("dp", "expert"), None),
        P(("dp", "expert"), None),
        P(("dp", "expert")),
        P(),
        P(None, "expert", "dp"),
        P(None, "expert", "dp"),
        P(None, "expert", "dp"),
    )
    return jax.shard_map(
        local,
        mesh=mesh,
        in_specs=placed,
        out_specs=(
            P(("dp", "expert"), None),
            P(None, "expert", "dp"),
            P(None, "expert", "dp"),
            P(None, "expert", "dp"),
        ),
        check_vma=False,
    )
```

```python
import functools

import jax
import jax.numpy as jnp
from jax import lax
from jax.experimental import pallas as pl
from jax.experimental.pallas import tpu as pltpu
from jax.sharding import PartitionSpec as P

VMEM_BYTES = 56 * 1024 * 1024
ANY = pl.BlockSpec(memory_space=pl.ANY)
SMEM = pl.BlockSpec(memory_space=pltpu.SMEM)
VMEM = pl.BlockSpec(memory_space=pltpu.VMEM)
CONTRACT_LAST = (((1,), (1,)), ((), ()))
KINDS = 3


def xor(a, b):
    return jnp.bitwise_xor(a, b)


def swap(value, mask):
    size = lax.axis_size("expert")
    return lax.ppermute(value, "expert", [(i, i ^ mask) for i in range(size)])


def axis_bits(size):
    return [1 << b for b in range(size.bit_length() - 1)]


def hop(value, turn):
    parts, slots = lax.axis_size("dp"), lax.axis_size("expert")
    bits = axis_bits(parts)
    pairs = []
    for d in range(parts):
        for e in range(slots):
            bit = (bits if e % 2 == 0 else bits[::-1])[turn]
            pairs.append((d * slots + e, (d ^ bit) * slots + e))
    return lax.ppermute(value, ("dp", "expert"), pairs)


def feature_block(parts, j):
    bits = axis_bits(parts)
    even = sum(b for t, b in enumerate(bits) if j >> t & 1)
    odd = sum(b for t, b in enumerate(bits[::-1]) if j >> t & 1)
    mask = jnp.where(lax.axis_index("expert") % 2 == 0, even, odd)
    return xor(lax.axis_index("dp"), mask)


def params():
    return pltpu.CompilerParams(vmem_limit_bytes=VMEM_BYTES)


def cost(flops, nbytes, trans=0):
    return pl.CostEstimate(flops=flops, bytes_accessed=nbytes, transcendentals=trans)


def run(copies):
    for copy in copies:
        copy.start()
    for copy in copies:
        copy.wait()


def pick_kernel(wanted, assign, *rest):
    weights, outs = rest[:KINDS], rest[KINDS:-2]
    stage, sems = rest[-2:]
    me = lax.axis_index("expert")
    loads, stores = [], []
    for out, chunks in zip(outs, wanted):
        first = len(loads)
        for s, k in chunks:
            chosen = assign[s, xor(me, k)]
            n = len(loads)
            loads.append(
                [
                    pltpu.make_async_copy(ref.at[chosen], stage.at[n, w], sems.at[n, w])
                    for w, ref in enumerate(weights)
                ]
            )
        stores.append(
            (
                first,
                len(chunks),
                pltpu.make_async_copy(
                    stage.at[pl.ds(first, len(chunks))], out, sems.at[first, KINDS]
                ),
            )
        )
    for load in loads:
        for copy in load:
            copy.start()
    for first, count, store in stores:
        for load in loads[first : first + count]:
            for copy in load:
                copy.wait()
        store.start()
    for _, _, store in stores:
        store.wait()


def pick(wanted, assign, weights):
    chunk = (KINDS,) + weights[0].shape[1:]
    dtype = weights[0].dtype
    count = sum(map(len, wanted))
    return pl.pallas_call(
        functools.partial(pick_kernel, wanted),
        out_shape=[jax.ShapeDtypeStruct((len(chunks),) + chunk, dtype) for chunks in wanted],
        in_specs=[SMEM] + [ANY] * KINDS,
        out_specs=[ANY] * len(wanted),
        scratch_shapes=[
            pltpu.VMEM((count,) + chunk, dtype),
            pltpu.SemaphoreType.DMA((count, KINDS + 1)),
        ],
        compiler_params=params(),
        cost_estimate=cost(0, 4 * count * chunk[0] * chunk[1] * chunk[2]),
        name="pick",
    )(assign, *weights)


def weight_loads(pieces, kept, target, sems, first):
    parts = lax.axis_size("dp")
    copies = []
    for ref, n, j, position in pieces:
        units, width = ref.shape[2], ref.shape[3]
        at = pl.multiple_of(feature_block(parts, j) * width, width)
        copies.append(
            pltpu.make_async_copy(
                ref.at[n, pl.ds(0, kept)],
                target.at[:, pl.ds(position * units, units), pl.ds(at, width)],
                sems.at[first + len(copies)],
            )
        )
    return copies


def bind(table, refs):
    return [(refs[a], n, j, position) for a, n, j, position in table]


def act_kernel(step, batches, table, count, counts, tokens, upstream, *rest):
    pieces = bind(table, rest[:count])
    hidden, gate_grad, up_grad, weights, x, g, pre, sems = rest[count:]
    rows = x.shape[0]
    run(
        [
            pltpu.make_async_copy(tokens.at[pl.ds(step * rows, rows)], x, sems.at[0]),
            pltpu.make_async_copy(upstream.at[pl.ds(step * rows, rows)], g, sems.at[1]),
        ]
        + weight_loads(pieces, KINDS, weights, sems, 2)
    )
    width = pre.shape[2]
    batch_rows = rows // batches
    for at in range(0, hidden.shape[1], width):
        cols = pl.ds(at, width)
        for w, left in enumerate((x, x, g)):
            pre[w] = lax.dot_general(
                left[...], weights[w, cols, :], CONTRACT_LAST, preferred_element_type=jnp.float32
            )
        for b in range(batches):
            span = pl.ds(b * batch_rows, batch_rows)
            live = (
                lax.broadcasted_iota(jnp.int32, (batch_rows, width), 0)
                < counts[step * batches + b]
            )
            gate_pre, up_pre, hidden_grad = pre[0, span, :], pre[1, span, :], pre[2, span, :]
            sigmoid = jax.nn.sigmoid(gate_pre)
            active = gate_pre * sigmoid
            kept = jnp.where(live, hidden_grad, 0.0)
            hidden[span, cols] = jnp.where(live, active * up_pre, 0.0).astype(hidden.dtype)
            gate_grad[span, cols] = (
                kept * up_pre * sigmoid * (1.0 + gate_pre * (1.0 - sigmoid))
            ).astype(gate_grad.dtype)
            up_grad[span, cols] = (kept * active).astype(up_grad.dtype)


def act(step, rows, units, batches, counts, tokens, upstream, table, arrays):
    features = tokens.shape[1]
    out = jax.ShapeDtypeStruct((rows, units), tokens.dtype)
    width = min(units, 256)
    return pl.pallas_call(
        functools.partial(act_kernel, step, batches, table, len(arrays)),
        out_shape=[out] * 3,
        in_specs=[SMEM, ANY, ANY] + [ANY] * len(arrays),
        out_specs=[VMEM] * 3,
        scratch_shapes=[
            pltpu.VMEM((KINDS, units, features), tokens.dtype),
            pltpu.VMEM((rows, features), tokens.dtype),
            pltpu.VMEM((rows, features), tokens.dtype),
            pltpu.VMEM((3, rows, width), jnp.float32),
            pltpu.SemaphoreType.DMA((2 + len(table),)),
        ],
        compiler_params=params(),
        cost_estimate=cost(
            6 * rows * units * features, 2 * (2 * rows + 3 * units) * features, rows * units
        ),
        name="act",
    )(counts, tokens, upstream, *arrays)


def weight_grads_kernel(step, scale, groups, tokens, upstream, hidden, gate_grad, up_grad, *rest):
    x, g, turned, stage, sems = rest[-5:]
    outs = rest[:-5]
    parts, rows, width = x.shape
    chunk = outs[0].shape[2]
    order = list(range(parts))[::-1]
    loads = {}
    for j in order:
        at = pl.multiple_of(feature_block(parts, j) * width, width)
        for n, (whole, local) in enumerate(((tokens, x), (upstream, g))):
            loads[j, n] = pltpu.make_async_copy(
                whole.at[pl.ds(step * rows, rows), pl.ds(at, width)],
                local.at[j],
                sems.at[2 * j + n],
            )
            loads[j, n].start()
    for w, ref in enumerate((gate_grad, up_grad, hidden)):
        turned[w] = ref[...].T
    stores = []
    for j in order:
        for w in range(KINDS):
            if w == 0:
                loads[j, 0].wait()
            if w == 2:
                loads[j, 1].wait()
            right = (x, x, g)[w]
            stage[j, w] = (
                jnp.dot(turned[w], right[j], preferred_element_type=jnp.float32) * scale
            ).astype(stage.dtype)
        for n, positions in enumerate(groups):
            for i, position in enumerate(positions):
                store = pltpu.make_async_copy(
                    stage.at[j, :, pl.ds(position * chunk, chunk), :],
                    outs[n * parts + j].at[i],
                    sems.at[2 * parts + len(stores)],
                )
                store.start()
                stores.append(store)
    for store in stores:
        store.wait()


def weight_grads(step, parts, chunk, scale, tokens, upstream, hidden, gate_grad, up_grad, groups):
    rows, units = hidden.shape
    features = tokens.shape[1]
    width = features // parts
    shapes = [
        jax.ShapeDtypeStruct((len(positions), KINDS, chunk, width), tokens.dtype)
        for positions in groups
        for _ in range(parts)
    ]
    stores = sum(map(len, groups)) * parts
    flat = pl.pallas_call(
        functools.partial(weight_grads_kernel, step, scale, groups),
        out_shape=shapes,
        in_specs=[ANY, ANY, VMEM, VMEM, VMEM],
        out_specs=[ANY] * len(shapes),
        scratch_shapes=[
            pltpu.VMEM((parts, rows, width), tokens.dtype),
            pltpu.VMEM((parts, rows, width), tokens.dtype),
            pltpu.VMEM((KINDS, units, rows), tokens.dtype),
            pltpu.VMEM((parts, KINDS, units, width), tokens.dtype),
            pltpu.SemaphoreType.DMA((2 * parts + stores,)),
        ],
        compiler_params=params(),
        cost_estimate=cost(6 * rows * units * features, 2 * (2 * rows + 3 * units) * features),
        name="weight_grads",
    )(tokens, upstream, hidden, gate_grad, up_grad)
    return [
        {j: flat[n * parts + j] for j in range(parts)} for n in range(len(groups))
    ]


def input_grad_kernel(step, table, count, has_base, gate_grad, up_grad, *rest):
    pieces = bind(table, rest[:count])
    out, weights, stage, sems = rest[count + has_base :]
    run(weight_loads(pieces, 2, weights, sems, 0))
    parts, rows, width = stage.shape
    stores = []
    for n in range(parts):
        cols = pl.ds(n * width, width)
        stage[n] = (
            jnp.dot(gate_grad[...], weights[0, :, cols], preferred_element_type=jnp.float32)
            + jnp.dot(up_grad[...], weights[1, :, cols], preferred_element_type=jnp.float32)
        ).astype(stage.dtype)
        store = pltpu.make_async_copy(
            stage.at[n], out.at[pl.ds(step * rows, rows), cols], sems.at[len(table) + n]
        )
        store.start()
        stores.append(store)
    for store in stores:
        store.wait()


def input_grad(step, steps, gate_grad, up_grad, table, arrays, features, base):
    rows, units = gate_grad.shape
    parts = max(1, features // 512)
    more = [] if base is None else [base]
    return pl.pallas_call(
        functools.partial(input_grad_kernel, step, table, len(arrays), len(more)),
        out_shape=jax.ShapeDtypeStruct((steps * rows, features), gate_grad.dtype),
        in_specs=[VMEM, VMEM] + [ANY] * (len(arrays) + len(more)),
        out_specs=ANY,
        scratch_shapes=[
            pltpu.VMEM((2, units, features), gate_grad.dtype),
            pltpu.VMEM((parts, rows, features // parts), gate_grad.dtype),
            pltpu.SemaphoreType.DMA((len(table) + parts,)),
        ],
        input_output_aliases={2 + len(arrays): 0} if more else {},
        compiler_params=params(),
        cost_estimate=cost(4 * rows * units * features, 2 * (rows + 2 * units) * features),
        name="input_grad",
    )(gate_grad, up_grad, *arrays, *more)


def place_kernel(table, count, assign, *rest):
    pieces = rest[:count]
    outs = rest[count:]
    me = lax.axis_index("expert")
    expert = pl.program_id(0)
    for out in outs:
        out[...] = jnp.zeros_like(out)
    for a, n, s, k in table:

        @pl.when(assign[s, xor(me, k)] == expert)
        def _():
            for w, out in enumerate(outs):
                out[0] += pieces[a][n, w].astype(jnp.float32)


def place(assign, home, experts):
    arrays = list({id(a): a for a, _, _, _ in home}.values())
    index = {id(a): i for i, a in enumerate(arrays)}
    table = tuple((index[id(a)], n, s, k) for a, n, s, k in home)
    units, width = arrays[0].shape[2:]
    out = jax.ShapeDtypeStruct((experts, units, width), jnp.float32)
    return pl.pallas_call(
        functools.partial(place_kernel, table, len(arrays)),
        grid=(experts,),
        out_shape=[out] * KINDS,
        in_specs=[SMEM] + [VMEM] * len(arrays),
        out_specs=[pl.BlockSpec((1, units, width), lambda e: (e, 0, 0))] * KINDS,
        compiler_params=params(),
        name="place",
    )(assign, *arrays)


def finish_kernel(table, count, assign, *rest):
    pieces = rest[:count]
    outs = rest[count + KINDS : count + 2 * KINDS]
    held, terms, sems = rest[count + 2 * KINDS :]
    me = lax.axis_index("expert")
    chosen = [assign[s, xor(me, k)] for _, _, s, k in table]
    first = []
    for m in range(len(table)):
        slot = jnp.int32(m)
        for o in range(m - 1, -1, -1):
            slot = jnp.where(chosen[o] == chosen[m], o, slot)
        first.append(slot)
    loads = [
        [pltpu.make_async_copy(pieces[a].at[n], terms.at[m], sems.at[m, KINDS])]
        + [
            pltpu.make_async_copy(outs[w].at[chosen[m]], held.at[m, w], sems.at[m, w])
            for w in range(KINDS)
        ]
        for m, (a, n, _, _) in enumerate(table)
    ]
    for load in loads:
        for copy in load:
            copy.start()
    for load in loads:
        for copy in load:
            copy.wait()
    for m in range(len(table)):
        held[first[m]] += terms[m].astype(jnp.float32)
    for wait in (False, True):
        for m in range(len(table)):

            @pl.when(first[m] == m)
            def _():
                for w in range(KINDS):
                    store = pltpu.make_async_copy(
                        held.at[m, w], outs[w].at[chosen[m]], sems.at[m, w]
                    )
                    store.wait() if wait else store.start()


def finish(assign, home, totals):
    arrays = list({id(a): a for a, _, _, _ in home}.values())
    index = {id(a): i for i, a in enumerate(arrays)}
    table = tuple((index[id(a)], n, s, k) for a, n, s, k in home)
    shape = totals[0].shape[1:]
    return pl.pallas_call(
        functools.partial(finish_kernel, table, len(arrays)),
        out_shape=[jax.ShapeDtypeStruct(t.shape, t.dtype) for t in totals],
        in_specs=[SMEM] + [ANY] * (len(arrays) + KINDS),
        out_specs=[ANY] * KINDS,
        scratch_shapes=[
            pltpu.VMEM((len(table), KINDS) + shape, jnp.float32),
            pltpu.VMEM((len(table), KINDS) + shape, arrays[0].dtype),
            pltpu.SemaphoreType.DMA((len(table), KINDS + 1)),
        ],
        input_output_aliases={1 + len(arrays) + w: w for w in range(KINDS)},
        compiler_params=params(),
        name="finish",
    )(assign, *arrays, *totals)


class Line:
    def __init__(self, depth):
        self.depth = depth
        self.sent = []
        self.gates = {}
        self.plans = []

    def send(self, move, value, *way, behind=()):
        gate = self.gates.get(len(self.sent), [])
        behind = list(behind) + list(gate() if callable(gate) else gate)
        depth = self.depth
        behind += self.sent[:-depth][-1:] + self.sent[: 1 - depth][-1:]
        if behind:
            value = after(value, *behind)
        self.sent.append(move(value, *way))
        result = self.sent[-1]
        self.settle()
        return result

    def settle(self, everything=False):
        while self.plans and (everything or self.plans[0][0] < len(self.sent)):
            number, plan = self.plans.pop(0)
            plan(self.sent[min(number, len(self.sent) - 1)])

    def plan(self, lag, what):
        self.plans.append((len(self.sent) - 1 + lag, what))
        self.plans.sort(key=lambda item: item[0])


def after(value, *others):
    return lax.optimization_barrier((value, *others))[0]


def overlap(jobs, sends):
    before = None
    for job in jobs:
        next(job)
        if before is not None:
            next(before)
            next(before, None)
        for _ in range(sends - 2):
            next(job)
        before = job
    next(before)
    next(before, None)


def spread(line, own, done):
    have = {0: own}
    for turn in range(len(axis_bits(lax.axis_size("dp")))):
        have[1 << turn] = line.send(hop, own, turn)
        yield True
    for turn in range(len(axis_bits(lax.axis_size("dp")))):
        for j in sorted(have):
            if j and j < 1 << turn:
                have[j | 1 << turn] = line.send(hop, have[j], turn)
                yield True
    done(have)


def collect(line, produced, done):
    terms = {j: [a] for j, a in produced.items()}

    def total(addends):
        if len(addends) == 1:
            return addends[0]
        return sum(a.astype(jnp.float32) for a in addends).astype(addends[0].dtype)

    for turn in range(len(axis_bits(len(produced)))):
        for j in sorted([j for j in terms if j >> turn & 1], reverse=True):
            terms[j ^ 1 << turn].append(line.send(hop, total(terms.pop(j)), turn))
            yield True
    done(total(terms[0]))


def local(tokens, upstream, counts, assign, gate_weight, up_weight, down_weight):
    steps, slots = assign.shape
    rows = tokens.shape[0] // steps
    batches = counts.shape[0] // steps
    features = tokens.shape[1]
    experts, chunk, _ = gate_weight.shape
    parts = lax.axis_size("dp")
    units = slots * chunk
    weights = (gate_weight, up_weight, down_weight)
    every = range(steps)
    far = slots // 2
    near = [k for k in range(2, slots, 2) if k != far][::-1]
    remote = near + [far]
    position = {k: 2 * i for i, k in enumerate([0] + remote)}
    wide, deep = Line(3), Line(2)

    moves = [(s, k) for s in every for k in remote]
    pairs = [((s, k), (s, k ^ 1)) for s, k in moves]
    own, mate, *messages = pick(
        (tuple((s, 0) for s in every), tuple((s, 1) for s in every), *pairs[: len(near)]),
        assign,
        weights,
    )
    mate = swap(mate, 1)
    wide.plan(
        1,
        lambda arrival: messages.extend(
            pick(tuple(pairs[len(near) :]), after(assign, arrival), weights)
        ),
    )

    arrived = {}

    def beside(s, k):
        return (3 + 6 * s if k == far else 5 * s) * (parts - 1) // 3

    def fetch(key):
        while key not in arrived:
            s, k = moves[len(deep.sent)]
            behind = []
            if s or k == far:
                behind = wide.sent[: beside(s, k) + 1][-3:]
                behind += [arrived[s, near[0]] if k == far and near else arrived[s - 1, far]]
            arrived[s, k] = deep.send(swap, messages[len(deep.sent)], k, behind=behind)

    def ahead(arrival):
        n = len(deep.sent)
        if n < len(moves) and beside(*moves[n]) < len(wide.sent):
            fetch(moves[n])
        wide.plan(1, ahead)

    ready = []
    table = [[] for _ in every]

    def deliver(keys, array, places):
        for key in keys:
            fetch(key)
        if keys:
            pairs = [arrived[key] for key in keys]
            theirs = [pair[1:] for pair in pairs]
            theirs = theirs[0] if len(theirs) == 1 else jnp.concatenate(theirs)
            theirs = after(theirs, *wide.sent[-3:], *messages[len(near) :][:1])
            array = jnp.concatenate([pair[:1] for pair in pairs] + [swap(theirs, 1)])
            ready.append(array)

        def done(have):
            for j, a in have.items():
                for n, (s, p) in enumerate(places):
                    table[s].append((a, n, j, p))

        yield from spread(wide, array, done)

    jobs = [
        deliver([], own, [(s, 0) for s in every]),
        deliver([], mate, [(s, 1) for s in every]),
    ]
    for s in every:
        for group in (near, [far]):
            if group:
                places = [(s, position[k] + c) for c in range(2) for k in group]
                jobs.append(deliver([(s, k) for k in group], None, places))
    for k in near:
        fetch((0, k))
    wide.plan(1, ahead)
    overlap(jobs, parts - 1)
    wide.plans.clear()

    counts = after(counts, ready[-1])
    token_grad = None
    early, late, totals = [], [], []
    jobs = []
    for s in every:
        arrays = list({id(a): a for a, _, _, _ in table[s]}.values())
        index = {id(a): i for i, a in enumerate(arrays)}
        places = tuple((index[id(a)], n, j, p) for a, n, j, p in table[s])
        hidden, gate_grad, up_grad = act(
            s, rows, units, batches, counts, tokens, upstream, places, arrays
        )
        if s == 0:
            hidden = after(hidden, wide.sent[-parts])
        groups = [g for g in ([far], near) if g]
        produced = weight_grads(
            s, parts, chunk, 1.0 / rows, tokens, upstream, hidden, gate_grad, up_grad,
            tuple(
                tuple(position[k] + c for k in group for c in range(2)) for group in groups + [[0]]
            ),
        )
        token_grad = input_grad(
            s, steps, gate_grad, up_grad, places, arrays, features, token_grad
        )
        jobs.append([(s, group, terms) for group, terms in zip(groups + [[0]], produced)])

    def returned(s, group):
        home = late if s == steps - 1 or group == [0] else early

        def mates(pairs):
            def go(arrival):
                seconds = [pair[1:] for _, pair in pairs]
                seconds = seconds[0] if len(seconds) == 1 else jnp.concatenate(seconds)
                seconds = swap(seconds if arrival is None else after(seconds, arrival), 1)
                home.extend((seconds, n, s, k ^ 1) for n, (k, _) in enumerate(pairs))

            return go

        def done(total):
            pairs = []
            for i, k in enumerate(group):
                pair = total[2 * i : 2 * i + 2]
                if k:
                    pair = deep.send(swap, pair, k)
                home.append((pair, 0, s, k))
                pairs.append((k, pair))
            if group == [0]:
                mates(pairs)(None)
            else:
                wide.plan(parts - 1, mates(pairs))

        return done

    base = len(wide.sent)
    wide.gates[base + parts - 2] = [wide.sent[-1]]
    wide.gates[base + parts] = [wide.sent[-1]]
    remote_jobs = [job for step in jobs for job in step[:-1]]
    own_jobs = [step[-1] for step in jobs]
    jobs = [
        collect(wide, terms, returned(s, group)) for s, group, terms in remote_jobs + own_jobs
    ]
    def place_early():
        totals.extend(place(assign, early, experts))
        return totals

    back = len(moves)
    wide.gates[base + 2 * parts - 3] = lambda: [deep.sent[back], wide.sent[-1]]
    wide.gates[base + 4 * parts - 6] = lambda: [
        token_grad,
        *deep.sent[back + 1 : back + 1 + len(near)],
    ]
    wide.gates[base + 4 * parts - 3] = lambda: [deep.sent[back + 1 + len(near)]]
    wide.gates[base + 4 * parts - 2] = place_early
    wide.gates[base + 4 * parts + 1] = lambda: deep.sent[back + 2 + len(near) :][:1]
    overlap(jobs, parts - 1)
    wide.settle(True)
    totals = finish(assign, late, totals)
    return (token_grad, *totals)


def solution(mesh):
    placed = (
        P(("dp", "expert"), None),
        P(("dp", "expert"), None),
        P(("dp", "expert")),
        P(),
        P(None, "expert", "dp"),
        P(None, "expert", "dp"),
        P(None, "expert", "dp"),
    )
    return jax.shard_map(
        local,
        mesh=mesh,
        in_specs=placed,
        out_specs=(
            P(("dp", "expert"), None),
            P(None, "expert", "dp"),
            P(None, "expert", "dp"),
            P(None, "expert", "dp"),
        ),
        check_vma=False,
    )
```

```python
import functools

import jax
import jax.numpy as jnp
from jax import lax
from jax.experimental import pallas as pl
from jax.experimental.pallas import tpu as pltpu
from jax.sharding import PartitionSpec as P

VMEM_BYTES = 56 * 1024 * 1024
ANY = pl.BlockSpec(memory_space=pl.ANY)
SMEM = pl.BlockSpec(memory_space=pltpu.SMEM)
VMEM = pl.BlockSpec(memory_space=pltpu.VMEM)
CONTRACT_LAST = (((1,), (1,)), ((), ()))
KINDS = 3


def xor(a, b):
    return jnp.bitwise_xor(a, b)


def swap(value, mask):
    size = lax.axis_size("expert")
    return lax.ppermute(value, "expert", [(i, i ^ mask) for i in range(size)])


def axis_bits(size):
    return [1 << b for b in range(size.bit_length() - 1)]


def hop(value, turn):
    parts, slots = lax.axis_size("dp"), lax.axis_size("expert")
    bits = axis_bits(parts)
    pairs = []
    for d in range(parts):
        for e in range(slots):
            bit = (bits if e % 2 == 0 else bits[::-1])[turn]
            pairs.append((d * slots + e, (d ^ bit) * slots + e))
    return lax.ppermute(value, ("dp", "expert"), pairs)


def feature_block(parts, j):
    bits = axis_bits(parts)
    even = sum(b for t, b in enumerate(bits) if j >> t & 1)
    odd = sum(b for t, b in enumerate(bits[::-1]) if j >> t & 1)
    mask = jnp.where(lax.axis_index("expert") % 2 == 0, even, odd)
    return xor(lax.axis_index("dp"), mask)


def params():
    return pltpu.CompilerParams(vmem_limit_bytes=VMEM_BYTES)


def cost(flops, nbytes, trans=0):
    return pl.CostEstimate(flops=flops, bytes_accessed=nbytes, transcendentals=trans)


def run(copies):
    for copy in copies:
        copy.start()
    for copy in copies:
        copy.wait()


def pick_kernel(wanted, assign, *rest):
    weights, outs = rest[:KINDS], rest[KINDS:-2]
    stage, sems = rest[-2:]
    me = lax.axis_index("expert")
    loads, stores = [], []
    for out, chunks in zip(outs, wanted):
        first = len(loads)
        for s, k in chunks:
            chosen = assign[s, xor(me, k)]
            n = len(loads)
            loads.append(
                [
                    pltpu.make_async_copy(ref.at[chosen], stage.at[n, w], sems.at[n, w])
                    for w, ref in enumerate(weights)
                ]
            )
        stores.append(
            (
                first,
                len(chunks),
                pltpu.make_async_copy(
                    stage.at[pl.ds(first, len(chunks))], out, sems.at[first, KINDS]
                ),
            )
        )
    for load in loads:
        for copy in load:
            copy.start()
    for first, count, store in stores:
        for load in loads[first : first + count]:
            for copy in load:
                copy.wait()
        store.start()
    for _, _, store in stores:
        store.wait()


def pick(wanted, assign, weights):
    chunk = (KINDS,) + weights[0].shape[1:]
    dtype = weights[0].dtype
    count = sum(map(len, wanted))
    return pl.pallas_call(
        functools.partial(pick_kernel, wanted),
        out_shape=[jax.ShapeDtypeStruct((len(chunks),) + chunk, dtype) for chunks in wanted],
        in_specs=[SMEM] + [ANY] * KINDS,
        out_specs=[ANY] * len(wanted),
        scratch_shapes=[
            pltpu.VMEM((count,) + chunk, dtype),
            pltpu.SemaphoreType.DMA((count, KINDS + 1)),
        ],
        compiler_params=params(),
        cost_estimate=cost(0, 4 * count * chunk[0] * chunk[1] * chunk[2]),
        name="pick",
    )(assign, *weights)


def weight_loads(pieces, kept, target, sems, first):
    parts = lax.axis_size("dp")
    copies = []
    for ref, n, j, position in pieces:
        units, width = ref.shape[2], ref.shape[3]
        at = pl.multiple_of(feature_block(parts, j) * width, width)
        copies.append(
            pltpu.make_async_copy(
                ref.at[n, pl.ds(0, kept)],
                target.at[:, pl.ds(position * units, units), pl.ds(at, width)],
                sems.at[first + len(copies)],
            )
        )
    return copies


def bind(table, refs):
    return [(refs[a], n, j, position) for a, n, j, position in table]


def act_kernel(step, batches, table, count, counts, tokens, upstream, *rest):
    pieces = bind(table, rest[:count])
    hidden, gate_grad, up_grad, weights, x, g, pre, sems = rest[count:]
    rows = x.shape[0]
    run(
        [
            pltpu.make_async_copy(tokens.at[pl.ds(step * rows, rows)], x, sems.at[0]),
            pltpu.make_async_copy(upstream.at[pl.ds(step * rows, rows)], g, sems.at[1]),
        ]
        + weight_loads(pieces, KINDS, weights, sems, 2)
    )
    width = pre.shape[2]
    batch_rows = rows // batches
    for at in range(0, hidden.shape[1], width):
        cols = pl.ds(at, width)
        for w, left in enumerate((x, x, g)):
            pre[w] = lax.dot_general(
                left[...], weights[w, cols, :], CONTRACT_LAST, preferred_element_type=jnp.float32
            )
        for b in range(batches):
            span = pl.ds(b * batch_rows, batch_rows)
            live = (
                lax.broadcasted_iota(jnp.int32, (batch_rows, width), 0)
                < counts[step * batches + b]
            )
            gate_pre, up_pre, hidden_grad = pre[0, span, :], pre[1, span, :], pre[2, span, :]
            sigmoid = jax.nn.sigmoid(gate_pre)
            active = gate_pre * sigmoid
            kept = jnp.where(live, hidden_grad, 0.0)
            hidden[span, cols] = jnp.where(live, active * up_pre, 0.0).astype(hidden.dtype)
            gate_grad[span, cols] = (
                kept * up_pre * sigmoid * (1.0 + gate_pre * (1.0 - sigmoid))
            ).astype(gate_grad.dtype)
            up_grad[span, cols] = (kept * active).astype(up_grad.dtype)


def act(step, rows, units, batches, counts, tokens, upstream, table, arrays):
    features = tokens.shape[1]
    out = jax.ShapeDtypeStruct((rows, units), tokens.dtype)
    width = min(units, 256)
    return pl.pallas_call(
        functools.partial(act_kernel, step, batches, table, len(arrays)),
        out_shape=[out] * 3,
        in_specs=[SMEM, ANY, ANY] + [ANY] * len(arrays),
        out_specs=[VMEM] * 3,
        scratch_shapes=[
            pltpu.VMEM((KINDS, units, features), tokens.dtype),
            pltpu.VMEM((rows, features), tokens.dtype),
            pltpu.VMEM((rows, features), tokens.dtype),
            pltpu.VMEM((3, rows, width), jnp.float32),
            pltpu.SemaphoreType.DMA((2 + len(table),)),
        ],
        compiler_params=params(),
        cost_estimate=cost(
            6 * rows * units * features, 2 * (2 * rows + 3 * units) * features, rows * units
        ),
        name="act",
    )(counts, tokens, upstream, *arrays)


def weight_grads_kernel(step, scale, groups, tokens, upstream, hidden, gate_grad, up_grad, *rest):
    x, g, turned, stage, sems = rest[-5:]
    outs = rest[:-5]
    parts, rows, width = x.shape
    chunk = outs[0].shape[2]
    order = list(range(parts))[::-1]
    loads = {}
    for j in order:
        at = pl.multiple_of(feature_block(parts, j) * width, width)
        for n, (whole, local) in enumerate(((tokens, x), (upstream, g))):
            loads[j, n] = pltpu.make_async_copy(
                whole.at[pl.ds(step * rows, rows), pl.ds(at, width)],
                local.at[j],
                sems.at[2 * j + n],
            )
            loads[j, n].start()
    for w, ref in enumerate((gate_grad, up_grad, hidden)):
        turned[w] = ref[...].T
    stores = []
    for j in order:
        for w in range(KINDS):
            if w == 0:
                loads[j, 0].wait()
            if w == 2:
                loads[j, 1].wait()
            right = (x, x, g)[w]
            stage[j, w] = (
                jnp.dot(turned[w], right[j], preferred_element_type=jnp.float32) * scale
            ).astype(stage.dtype)
        for n, positions in enumerate(groups):
            for i, position in enumerate(positions):
                store = pltpu.make_async_copy(
                    stage.at[j, :, pl.ds(position * chunk, chunk), :],
                    outs[n * parts + j].at[i],
                    sems.at[2 * parts + len(stores)],
                )
                store.start()
                stores.append(store)
    for store in stores:
        store.wait()


def weight_grads(step, parts, chunk, scale, tokens, upstream, hidden, gate_grad, up_grad, groups):
    rows, units = hidden.shape
    features = tokens.shape[1]
    width = features // parts
    shapes = [
        jax.ShapeDtypeStruct((len(positions), KINDS, chunk, width), tokens.dtype)
        for positions in groups
        for _ in range(parts)
    ]
    stores = sum(map(len, groups)) * parts
    flat = pl.pallas_call(
        functools.partial(weight_grads_kernel, step, scale, groups),
        out_shape=shapes,
        in_specs=[ANY, ANY, VMEM, VMEM, VMEM],
        out_specs=[ANY] * len(shapes),
        scratch_shapes=[
            pltpu.VMEM((parts, rows, width), tokens.dtype),
            pltpu.VMEM((parts, rows, width), tokens.dtype),
            pltpu.VMEM((KINDS, units, rows), tokens.dtype),
            pltpu.VMEM((parts, KINDS, units, width), tokens.dtype),
            pltpu.SemaphoreType.DMA((2 * parts + stores,)),
        ],
        compiler_params=params(),
        cost_estimate=cost(6 * rows * units * features, 2 * (2 * rows + 3 * units) * features),
        name="weight_grads",
    )(tokens, upstream, hidden, gate_grad, up_grad)
    return [
        {j: flat[n * parts + j] for j in range(parts)} for n in range(len(groups))
    ]


def input_grad_kernel(step, table, count, has_base, gate_grad, up_grad, *rest):
    pieces = bind(table, rest[:count])
    out, weights, stage, sems = rest[count + has_base :]
    run(weight_loads(pieces, 2, weights, sems, 0))
    parts, rows, width = stage.shape
    stores = []
    for n in range(parts):
        cols = pl.ds(n * width, width)
        stage[n] = (
            jnp.dot(gate_grad[...], weights[0, :, cols], preferred_element_type=jnp.float32)
            + jnp.dot(up_grad[...], weights[1, :, cols], preferred_element_type=jnp.float32)
        ).astype(stage.dtype)
        store = pltpu.make_async_copy(
            stage.at[n], out.at[pl.ds(step * rows, rows), cols], sems.at[len(table) + n]
        )
        store.start()
        stores.append(store)
    for store in stores:
        store.wait()


def input_grad(step, steps, gate_grad, up_grad, table, arrays, features, base):
    rows, units = gate_grad.shape
    parts = max(1, features // 512)
    more = [] if base is None else [base]
    return pl.pallas_call(
        functools.partial(input_grad_kernel, step, table, len(arrays), len(more)),
        out_shape=jax.ShapeDtypeStruct((steps * rows, features), gate_grad.dtype),
        in_specs=[VMEM, VMEM] + [ANY] * (len(arrays) + len(more)),
        out_specs=ANY,
        scratch_shapes=[
            pltpu.VMEM((2, units, features), gate_grad.dtype),
            pltpu.VMEM((parts, rows, features // parts), gate_grad.dtype),
            pltpu.SemaphoreType.DMA((len(table) + parts,)),
        ],
        input_output_aliases={2 + len(arrays): 0} if more else {},
        compiler_params=params(),
        cost_estimate=cost(4 * rows * units * features, 2 * (rows + 2 * units) * features),
        name="input_grad",
    )(gate_grad, up_grad, *arrays, *more)


def place_kernel(table, count, assign, *rest):
    pieces = rest[:count]
    outs = rest[count:]
    me = lax.axis_index("expert")
    expert = pl.program_id(0)
    for out in outs:
        out[...] = jnp.zeros_like(out)
    for a, n, s, k in table:

        @pl.when(assign[s, xor(me, k)] == expert)
        def _():
            for w, out in enumerate(outs):
                out[0] += pieces[a][n, w].astype(jnp.float32)


def place(assign, home, experts):
    arrays = list({id(a): a for a, _, _, _ in home}.values())
    index = {id(a): i for i, a in enumerate(arrays)}
    table = tuple((index[id(a)], n, s, k) for a, n, s, k in home)
    units, width = arrays[0].shape[2:]
    out = jax.ShapeDtypeStruct((experts, units, width), jnp.float32)
    return pl.pallas_call(
        functools.partial(place_kernel, table, len(arrays)),
        grid=(experts,),
        out_shape=[out] * KINDS,
        in_specs=[SMEM] + [VMEM] * len(arrays),
        out_specs=[pl.BlockSpec((1, units, width), lambda e: (e, 0, 0))] * KINDS,
        compiler_params=params(),
        name="place",
    )(assign, *arrays)


def finish_kernel(table, count, assign, *rest):
    pieces = rest[:count]
    outs = rest[count + KINDS : count + 2 * KINDS]
    held, terms, sems = rest[count + 2 * KINDS :]
    me = lax.axis_index("expert")
    chosen = [assign[s, xor(me, k)] for _, _, s, k in table]
    first = []
    for m in range(len(table)):
        slot = jnp.int32(m)
        for o in range(m - 1, -1, -1):
            slot = jnp.where(chosen[o] == chosen[m], o, slot)
        first.append(slot)
    loads = [
        [pltpu.make_async_copy(pieces[a].at[n], terms.at[m], sems.at[m, KINDS])]
        + [
            pltpu.make_async_copy(outs[w].at[chosen[m]], held.at[m, w], sems.at[m, w])
            for w in range(KINDS)
        ]
        for m, (a, n, _, _) in enumerate(table)
    ]
    for load in loads:
        for copy in load:
            copy.start()
    for load in loads:
        for copy in load:
            copy.wait()
    for m in range(len(table)):
        held[first[m]] += terms[m].astype(jnp.float32)
    for wait in (False, True):
        for m in range(len(table)):

            @pl.when(first[m] == m)
            def _():
                for w in range(KINDS):
                    store = pltpu.make_async_copy(
                        held.at[m, w], outs[w].at[chosen[m]], sems.at[m, w]
                    )
                    store.wait() if wait else store.start()


def finish(assign, home, totals):
    arrays = list({id(a): a for a, _, _, _ in home}.values())
    index = {id(a): i for i, a in enumerate(arrays)}
    table = tuple((index[id(a)], n, s, k) for a, n, s, k in home)
    shape = totals[0].shape[1:]
    return pl.pallas_call(
        functools.partial(finish_kernel, table, len(arrays)),
        out_shape=[jax.ShapeDtypeStruct(t.shape, t.dtype) for t in totals],
        in_specs=[SMEM] + [ANY] * (len(arrays) + KINDS),
        out_specs=[ANY] * KINDS,
        scratch_shapes=[
            pltpu.VMEM((len(table), KINDS) + shape, jnp.float32),
            pltpu.VMEM((len(table), KINDS) + shape, arrays[0].dtype),
            pltpu.SemaphoreType.DMA((len(table), KINDS + 1)),
        ],
        input_output_aliases={1 + len(arrays) + w: w for w in range(KINDS)},
        compiler_params=params(),
        name="finish",
    )(assign, *arrays, *totals)


class Line:
    def __init__(self, depth):
        self.depth = depth
        self.sent = []
        self.gates = {}
        self.plans = []

    def send(self, move, value, *way, behind=()):
        gate = self.gates.get(len(self.sent), [])
        behind = list(behind) + list(gate() if callable(gate) else gate)
        depth = self.depth
        behind += self.sent[:-depth][-1:] + self.sent[: 1 - depth][-1:]
        if behind:
            value = after(value, *behind)
        self.sent.append(move(value, *way))
        result = self.sent[-1]
        self.settle()
        return result

    def settle(self, everything=False):
        while self.plans and (everything or self.plans[0][0] < len(self.sent)):
            number, plan = self.plans.pop(0)
            plan(self.sent[min(number, len(self.sent) - 1)])

    def plan(self, lag, what):
        self.plans.append((len(self.sent) - 1 + lag, what))
        self.plans.sort(key=lambda item: item[0])


def after(value, *others):
    return lax.optimization_barrier((value, *others))[0]


def overlap(jobs, sends):
    before = None
    for job in jobs:
        next(job)
        if before is not None:
            next(before)
            next(before, None)
        for _ in range(sends - 2):
            next(job)
        before = job
    next(before)
    next(before, None)


def spread(line, own, done):
    have = {0: own}
    for turn in range(len(axis_bits(lax.axis_size("dp")))):
        have[1 << turn] = line.send(hop, own, turn)
        yield True
    for turn in range(len(axis_bits(lax.axis_size("dp")))):
        for j in sorted(have):
            if j and j < 1 << turn:
                have[j | 1 << turn] = line.send(hop, have[j], turn)
                yield True
    done(have)


def collect(line, produced, done):
    terms = {j: [a] for j, a in produced.items()}

    def total(addends):
        if len(addends) == 1:
            return addends[0]
        return sum(a.astype(jnp.float32) for a in addends).astype(addends[0].dtype)

    for turn in range(len(axis_bits(len(produced)))):
        for j in sorted([j for j in terms if j >> turn & 1], reverse=True):
            terms[j ^ 1 << turn].append(line.send(hop, total(terms.pop(j)), turn))
            yield True
    done(total(terms[0]))


def local(tokens, upstream, counts, assign, gate_weight, up_weight, down_weight):
    steps, slots = assign.shape
    rows = tokens.shape[0] // steps
    batches = counts.shape[0] // steps
    features = tokens.shape[1]
    experts, chunk, _ = gate_weight.shape
    parts = lax.axis_size("dp")
    units = slots * chunk
    weights = (gate_weight, up_weight, down_weight)
    every = range(steps)
    far = slots // 2
    near = [k for k in range(2, slots, 2) if k != far][::-1]
    remote = near + [far]
    position = {k: 2 * i for i, k in enumerate([0] + remote)}
    wide, deep = Line(3), Line(2)

    moves = [(s, k) for s in every for k in remote]
    pairs = [((s, k), (s, k ^ 1)) for s, k in moves]
    own, mate, *messages = pick(
        (tuple((s, 0) for s in every), tuple((s, 1) for s in every), *pairs[: len(near)]),
        assign,
        weights,
    )
    mate = swap(mate, 1)
    wide.plan(
        1,
        lambda arrival: messages.extend(
            pick(tuple(pairs[len(near) :]), after(assign, arrival), weights)
        ),
    )

    arrived = {}

    def beside(s, k):
        return (3 + 6 * s if k == far else 5 * s) * (parts - 1) // 3

    def fetch(key):
        while key not in arrived:
            s, k = moves[len(deep.sent)]
            behind = []
            if s or k == far:
                behind = wide.sent[: beside(s, k) + 1][-3:]
                behind += [arrived[s, near[0]] if k == far and near else arrived[s - 1, far]]
            arrived[s, k] = deep.send(swap, messages[len(deep.sent)], k, behind=behind)

    def ahead(arrival):
        n = len(deep.sent)
        if n < len(moves) and beside(*moves[n]) < len(wide.sent):
            fetch(moves[n])
        wide.plan(1, ahead)

    ready = []
    table = [[] for _ in every]

    def deliver(keys, array, places):
        for key in keys:
            fetch(key)
        if keys:
            pairs = [arrived[key] for key in keys]
            theirs = [pair[1:] for pair in pairs]
            theirs = theirs[0] if len(theirs) == 1 else jnp.concatenate(theirs)
            theirs = after(theirs, *wide.sent[-3:], *messages[len(near) :][:1])
            array = jnp.concatenate([pair[:1] for pair in pairs] + [swap(theirs, 1)])
            ready.append(array)

        def done(have):
            for j, a in have.items():
                for n, (s, p) in enumerate(places):
                    table[s].append((a, n, j, p))

        yield from spread(wide, array, done)

    jobs = [
        deliver([], own, [(s, 0) for s in every]),
        deliver([], mate, [(s, 1) for s in every]),
    ]
    for s in every:
        for group in (near, [far]):
            if group:
                places = [(s, position[k] + c) for c in range(2) for k in group]
                jobs.append(deliver([(s, k) for k in group], None, places))
    for k in near:
        fetch((0, k))
    wide.plan(1, ahead)
    overlap(jobs, parts - 1)
    wide.plans.clear()

    counts = after(counts, ready[-1])
    token_grad = None
    early, late, totals = [], [], []
    jobs = []
    for s in every:
        arrays = list({id(a): a for a, _, _, _ in table[s]}.values())
        index = {id(a): i for i, a in enumerate(arrays)}
        places = tuple((index[id(a)], n, j, p) for a, n, j, p in table[s])
        hidden, gate_grad, up_grad = act(
            s, rows, units, batches, counts, tokens, upstream, places, arrays
        )
        if s == 0:
            hidden = after(hidden, wide.sent[-parts])
        groups = [g for g in ([far], near) if g]
        produced = weight_grads(
            s, parts, chunk, 1.0 / rows, tokens, upstream, hidden, gate_grad, up_grad,
            tuple(
                tuple(position[k] + c for k in group for c in range(2)) for group in groups + [[0]]
            ),
        )
        token_grad = input_grad(
            s, steps, gate_grad, up_grad, places, arrays, features, token_grad
        )
        jobs.append([(s, group, terms) for group, terms in zip(groups + [[0]], produced)])

    def returned(s, group):
        home = late if s == steps - 1 or group == [0] else early

        def mates(pairs):
            def go(arrival):
                seconds = [pair[1:] for _, pair in pairs]
                seconds = seconds[0] if len(seconds) == 1 else jnp.concatenate(seconds)
                seconds = swap(seconds if arrival is None else after(seconds, arrival), 1)
                home.extend((seconds, n, s, k ^ 1) for n, (k, _) in enumerate(pairs))

            return go

        def done(total):
            pairs = []
            for i, k in enumerate(group):
                pair = total[2 * i : 2 * i + 2]
                if k:
                    pair = deep.send(swap, pair, k)
                home.append((pair, 0, s, k))
                pairs.append((k, pair))
            if group == [0]:
                mates(pairs)(None)
            else:
                wide.plan(parts - 1, mates(pairs))

        return done

    base = len(wide.sent)
    wide.gates[base + parts - 2] = [wide.sent[-1]]
    wide.gates[base + parts] = [wide.sent[-1]]
    remote_jobs = [job for step in jobs for job in step[:-1]]
    own_jobs = [step[-1] for step in jobs]
    jobs = [
        collect(wide, terms, returned(s, group)) for s, group, terms in remote_jobs + own_jobs
    ]
    def place_early():
        totals.extend(place(assign, early, experts))
        return totals

    back = len(moves)
    wide.gates[base + 2 * parts - 3] = lambda: [wide.sent[-1]]
    wide.gates[base + 2 * parts] = lambda: [deep.sent[back]]
    wide.gates[base + parts - 1] = [hidden]
    wide.gates[base + 2 * parts - 2] = [produced[0][0]]
    wide.gates[base + 4 * parts - 6] = lambda: [
        token_grad,
        *deep.sent[back + 1 : back + 1 + len(near)],
    ]
    wide.gates[base + 4 * parts - 3] = lambda: [deep.sent[back + 1 + len(near)]]
    wide.gates[base + 4 * parts - 2] = place_early
    wide.gates[base + 4 * parts + 1] = lambda: deep.sent[back + 2 + len(near) :][:1]
    overlap(jobs, parts - 1)
    wide.settle(True)
    totals = finish(assign, late, totals)
    return (token_grad, *totals)


def solution(mesh):
    placed = (
        P(("dp", "expert"), None),
        P(("dp", "expert"), None),
        P(("dp", "expert")),
        P(),
        P(None, "expert", "dp"),
        P(None, "expert", "dp"),
        P(None, "expert", "dp"),
    )
    return jax.shard_map(
        local,
        mesh=mesh,
        in_specs=placed,
        out_specs=(
            P(("dp", "expert"), None),
            P(None, "expert", "dp"),
            P(None, "expert", "dp"),
            P(None, "expert", "dp"),
        ),
        check_vma=False,
    )
```
